512 devices in a mesh: replica: 16 (over z_lo, y), fsdp: 32 (over z_hi, x, core).
Axes of the slice: x: 4, y: 4, z: 16 (z_hi: 4, z_lo: 4; z = z_hi * 4 + z_lo), core: 2. Of those that a mesh axis runs over, the one named last changes fastest.
Arguments:
- weights: bfloat16 [16, 8192, 512], P('replica', 'fsdp'), may hold values from -0.0625 to 0.0625
- first_moment: float32 [16, 8192, 512], P('replica', 'fsdp'), may hold values from -0.09375 to 0.09375
- second_moment: float32 [16, 8192, 512], P('replica', 'fsdp'), may hold values from 2.4414062e-06 to 0.00024414062
- anchor: float32 [8192, 512], P(('fsdp', 'replica')), may hold values from -0.0625 to 0.0625
- momentum: float32 [8192, 512], P(('fsdp', 'replica')), may hold values from -0.03 to 0.03
- inputs: bfloat16 [16, 4096, 8192], P('replica', 'fsdp'), may hold values from -6 to 6
- targets: bfloat16 [16, 4096, 512], P('replica', 'fsdp'), may hold values from -6 to 6
- keep_mask: int32 [16, 4096], P('replica', 'fsdp'), may hold values 0 or 1
Outputs:
- new_weights: bfloat16 [16, 8192, 512], P('replica', 'fsdp')
- new_first: float32 [16, 8192, 512], P('replica', 'fsdp')
- new_anchor: float32 [8192, 512], P(('fsdp', 'replica'))
- new_momentum: float32 [8192, 512], P(('fsdp', 'replica'))
The draws below stay inside these ranges and needn't reach their ends.
All inputs are finite; a program needn't handle non-finite values. No bound on the sum of `keep_mask` on one device may be relied on, other than what follows from the above.
Results may differ from the reference program's by a relative error of at most 0.01.
Values may be sent and summed in bfloat16 or wider, within the bound.
No kernel may reach another device: no remote copies, remote signals or barrier semaphores. Data moves between devices by JAX's collectives and lax.ppermute only.
A program may use at most 64 MiB of HBM per device.

```python
import math
import jax
import jax.numpy as jnp
from jax import lax

D = 8192
KV = 512
TOK_REP = 4096
FEAT_DEV = 256
REPLICAS = 16
N_REPLICA = 16
N_FSDP = 32


def set_ends(array, own_key, smallest, top_value):
    extent = array.shape
    place = [jax.random.randint(jax.random.fold_in(own_key, axis), (), 0, extent[axis]) for axis in range(len(extent))]
    array = array.at[tuple(place)].set(smallest)
    longest = extent.index(max(extent))
    place[longest] = (place[longest] + 1) % extent[longest]
    return array.at[tuple(place)].set(top_value)


def steps_of(rng, dims, shards, smallest, largest):
    factor_of = 1.0
    for axis_at, shards_of in shards:
        draws = jax.random.uniform(jax.random.fold_in(jax.random.fold_in(rng, 6), axis_at), (shards_of,), jnp.float32, smallest / len(shards), largest / len(shards))
        factor_of = factor_of * jnp.repeat(jnp.exp(draws), dims[axis_at] // shards_of).reshape((-1,) + (1,) * (len(dims) - 1 - axis_at))
    return factor_of


def normal_values(own_key, extent, scale, bound, cuts=(), held_as=jnp.bfloat16):
    drawn = jax.random.normal(own_key, extent, jnp.float32) * scale
    if len(cuts) > 0:
        drawn = steps_of(own_key, extent, cuts, -0.22, 0.18) * drawn
    return jnp.clip(drawn, min=-bound, max=bound).astype(held_as)


def setup_inputs(seed: int = 0) -> dict:
    key_of = jax.random.split(jax.random.key(seed), 9)
    return {
        "weights": normal_values(key_of[0], (REPLICAS, D, KV), D ** -0.5, 0.0625, ((0, 16), (1, 32))),
        "first_moment": normal_values(key_of[1], (REPLICAS, D, KV), (TOK_REP ** -0.5), 0.09375, ((0, 16), (1, 32)), jnp.float32),
        "second_moment": jnp.clip(jnp.exp(math.log(0.00024414062) - 4.6051702 * jax.random.uniform(key_of[2], (REPLICAS, D, KV), jnp.float32) ** steps_of(key_of[2], (REPLICAS, D, KV), ((0, 16), (1, 32)), -0.2, 0.2)), 2.441406195430318e-06, 0.00024414062),
        "anchor": normal_values(key_of[3], (D, KV), D ** -0.5, 0.0625, ((0, 512),), jnp.float32),
        "momentum": normal_values(key_of[4], (D, KV), 0.005, 0.03, ((0, 512),), jnp.float32),
        "inputs": normal_values(key_of[5], (REPLICAS, TOK_REP, D), 1.0, 6.0, ((0, 16), (1, 32))),
        "targets": normal_values(key_of[6], (REPLICAS, TOK_REP, KV), 1.0, 6.0, ((0, 16), (1, 32))),
        "keep_mask": set_ends((jax.random.randint(key_of[7], (REPLICAS, TOK_REP), 0, 4) < 3).astype(jnp.int32), jax.random.fold_in(key_of[7], 1), 0, 1),
    }


BETA_FIRST = 0.9
BETA_SECOND = 0.95
EPSILON = 1e-08
INNER_RATE = 0.002
WEIGHT_DECAY = 0.1
OUTER_RATE = 0.7
NESTEROV = 0.9
MIXING = 0.5

def worker_step(packed):
    weight_now, first_now, second_now, tokens, goal_rows, keep_rows = packed
    token_blocks = tokens.reshape(TOK_REP, N_FSDP, FEAT_DEV).astype(jnp.float32)
    weight_blocks = weight_now.reshape(N_FSDP, FEAT_DEV, KV).astype(jnp.float32)
    partials = jnp.einsum('tbf,bfk->btk', token_blocks, weight_blocks)
    rounded = lax.optimization_barrier(partials.astype(jnp.bfloat16))
    projected = lax.optimization_barrier(jnp.sum(rounded.astype(jnp.float32), 0))
    residual = ((projected - goal_rows.astype(jnp.float32)) * keep_rows.astype(jnp.float32)[:, None] / TOK_REP).astype(jnp.bfloat16)
    gradient = jnp.dot(tokens.T, residual, preferred_element_type=jnp.float32)
    weight_f = weight_now.astype(jnp.float32)
    first_new = BETA_FIRST * first_now + (1.0 - BETA_FIRST) * gradient
    second_new = BETA_SECOND * second_now + (1.0 - BETA_SECOND) * gradient * gradient
    moved = weight_f - INNER_RATE * (first_new / (jnp.sqrt(second_new) + EPSILON) + WEIGHT_DECAY * weight_f)
    return (moved.astype(jnp.bfloat16), first_new)

def reference(weights, first_moment, second_moment, anchor, momentum, inputs, targets, keep_mask):
    inner, new_first = lax.map(worker_step, (weights, first_moment, second_moment, inputs, targets, keep_mask))
    weight_mean = lax.optimization_barrier(jnp.sum(weights.astype(jnp.float32), 0)) / N_REPLICA
    pseudo_grad = anchor - weight_mean
    new_momentum = NESTEROV * momentum + pseudo_grad
    new_anchor = anchor - OUTER_RATE * (pseudo_grad + NESTEROV * new_momentum)
    new_weights = ((1.0 - MIXING) * new_anchor[None] + MIXING * inner.astype(jnp.float32)).astype(jnp.bfloat16)
    return (new_weights, new_first, new_anchor, new_momentum)
```

```python
import jax
import jax.numpy as jnp
from jax import lax
from jax.experimental import pallas as pl
from jax.experimental.pallas import tpu as pltpu
from jax.sharding import PartitionSpec as P

BETA_FIRST = 0.9
BETA_SECOND = 0.95
EPSILON = 1e-08
INNER_RATE = 0.002
WEIGHT_DECAY = 0.1
OUTER_RATE = 0.7
NESTEROV = 0.9
MIXING = 0.5

SLABS = 4
PLANE = 8
PLANES = [[z * PLANE + i for i in range(PLANE)] for z in range(SLABS)]


def shift_z(value, step):
    pairs = [
        (z * PLANE + i, (z + step) % SLABS * PLANE + i)
        for z in range(SLABS)
        for i in range(PLANE)
    ]
    return lax.ppermute(value, "fsdp", pairs)


def pack_kernel(slab_ref, tokens_ref, packed_ref):
    width = packed_ref.shape[2]
    for i in range(PLANE):
        packed_ref[i] = tokens_ref[:, i * width : (i + 1) * width]


def pack(tokens, slabs, width):
    rows = tokens.shape[0]
    return pl.pallas_call(
        pack_kernel,
        out_shape=jax.ShapeDtypeStruct((PLANE, rows, SLABS * width), tokens.dtype),
        grid_spec=pltpu.PrefetchScalarGridSpec(
            num_scalar_prefetch=1,
            grid=(SLABS,),
            in_specs=[pl.BlockSpec((rows, PLANE * width), lambda k, s: (0, s[k]))],
            out_specs=pl.BlockSpec((PLANE, rows, width), lambda k, s: (0, 0, k)),
        ),
        name="pack_columns",
    )(slabs, tokens)


def project_kernel(x_ref, w0_ref, w1_ref, w2_ref, w3_ref, out_ref):
    width = w0_ref.shape[0]
    total = None
    for k, w_ref in enumerate((w0_ref, w1_ref, w2_ref, w3_ref)):
        part = jnp.dot(
            x_ref[:, k * width : (k + 1) * width],
            w_ref[...],
            preferred_element_type=jnp.float32,
        )
        total = part if total is None else total + part
    out_ref[...] = total.astype(out_ref.dtype)


def project(columns, pieces):
    out_width = pieces[0].shape[1]
    return pl.pallas_call(
        project_kernel,
        out_shape=jax.ShapeDtypeStruct((columns.shape[0], out_width), jnp.bfloat16),
        compiler_params=pltpu.CompilerParams(vmem_limit_bytes=32 << 20),
        name="project",
    )(columns, *pieces)


def shards(weights, first_moment, second_moment, anchor, momentum, inputs, targets, keep_mask):
    initial = weights[0]
    tokens = inputs[0]
    goal_rows = targets[0]
    mask_rows = keep_mask[0].astype(jnp.float32)[:, None]
    rows = tokens.shape[0]
    width, out_width = initial.shape
    token_count = rows * lax.axis_size("fsdp")
    workers = lax.axis_size("replica")
    half = width // 2
    slab = lax.axis_index("fsdp") // PLANE

    before = shift_z(initial, 1)
    after = shift_z(initial, -1)
    opposite = jnp.concatenate(
        [shift_z(before[:half], 1), shift_z(after[half:], -1)], axis=0
    )
    order = jnp.stack([slab, (slab + 3) % SLABS, (slab + 1) % SLABS, (slab + 2) % SLABS])

    packed = pack(tokens, order.astype(jnp.int32), width)
    columns = lax.all_to_all(packed, "fsdp", 0, 0, axis_index_groups=PLANES)
    columns = columns.reshape(PLANE * rows, SLABS * width)

    share_rows = anchor.shape[0]
    every = lax.all_to_all(
        initial.reshape(workers, share_rows, out_width), "replica", 0, 0
    )
    weight_mean = jnp.sum(every.astype(jnp.float32), 0) / workers
    pseudo_grad = anchor - weight_mean
    new_momentum = NESTEROV * momentum + pseudo_grad
    new_anchor = anchor - OUTER_RATE * (pseudo_grad + NESTEROV * new_momentum)
    block_anchor = lax.all_to_all(
        jnp.broadcast_to(new_anchor[None], (workers, share_rows, out_width)), "replica", 0, 0
    ).reshape(width, out_width)

    partials = project(columns, (initial, before, after, opposite))
    mine = lax.all_to_all(
        partials.reshape(PLANE, rows, out_width), "fsdp", 0, 0, axis_index_groups=PLANES
    )
    projected = jnp.sum(mine.astype(jnp.float32), 0)
    residual = ((projected - goal_rows.astype(jnp.float32)) * mask_rows / token_count).astype(
        jnp.bfloat16
    )
    residuals = lax.all_to_all(
        jnp.broadcast_to(residual[None], (PLANE, rows, out_width)),
        "fsdp",
        0,
        0,
        axis_index_groups=PLANES,
    ).reshape(PLANE * rows, out_width)
    gradients = lax.dot_general(
        columns, residuals, (((0,), (0,)), ((), ())), preferred_element_type=jnp.float32
    )
    own, to_before, to_after, far = jnp.split(gradients, SLABS, axis=0)
    far = far.astype(jnp.bfloat16)
    passing_up = shift_z(far[:half], 1).astype(jnp.float32)
    passing_down = shift_z(far[half:], -1).astype(jnp.float32)
    up = jnp.concatenate([to_after[:half] + passing_up, to_after[half:]], axis=0)
    down = jnp.concatenate([to_before[:half], to_before[half:] + passing_down], axis=0)
    from_before = shift_z(up.astype(jnp.bfloat16), 1)
    from_after = shift_z(down.astype(jnp.bfloat16), -1)
    gradient = own + (from_before.astype(jnp.float32) + from_after.astype(jnp.float32))

    weight_f = initial.astype(jnp.float32)
    first_new = BETA_FIRST * first_moment[0] + (1.0 - BETA_FIRST) * gradient
    second_new = BETA_SECOND * second_moment[0] + (1.0 - BETA_SECOND) * gradient * gradient
    moved = weight_f - INNER_RATE * (
        first_new / (jnp.sqrt(second_new) + EPSILON) + WEIGHT_DECAY * weight_f
    )
    inner_weight = moved.astype(jnp.bfloat16)
    mixed = ((1.0 - MIXING) * block_anchor + MIXING * inner_weight.astype(jnp.float32)).astype(
        jnp.bfloat16
    )
    return (mixed[None], first_new[None], new_anchor, new_momentum)


def solution(mesh):
    return jax.shard_map(
        shards,
        mesh=mesh,
        in_specs=(
            P("replica", "fsdp", None),
            P("replica", "fsdp", None),
            P("replica", "fsdp", None),
            P(("fsdp", "replica"), None),
            P(("fsdp", "replica"), None),
            P("replica", "fsdp", None),
            P("replica", "fsdp", None),
            P("replica", "fsdp"),
        ),
        out_specs=(
            P("replica", "fsdp", None),
            P("replica", "fsdp", None),
            P(("fsdp", "replica"), None),
            P(("fsdp", "replica"), None),
        ),
        check_vma=False,
    )
```

```python
import functools

import jax
import jax.numpy as jnp
from jax import lax
from jax.experimental import pallas as pl
from jax.experimental.pallas import tpu as pltpu
from jax.sharding import PartitionSpec as P

BETA_FIRST = 0.9
BETA_SECOND = 0.95
EPSILON = 1e-08
INNER_RATE = 0.002
WEIGHT_DECAY = 0.1
OUTER_RATE = 0.7
NESTEROV = 0.9
MIXING = 0.5

SLABS = 4
PLANE = 8
PARTS = 1
PLANES = [[z * PLANE + i for i in range(PLANE)] for z in range(SLABS)]


def shift_z(value, step):
    pairs = [
        (z * PLANE + i, (z + step) % SLABS * PLANE + i)
        for z in range(SLABS)
        for i in range(PLANE)
    ]
    return lax.ppermute(value, "fsdp", pairs)


def shift_replica(value, z_step, y_step):
    pairs = [
        (z * 4 + y, (z + z_step) % 4 * 4 + (y + y_step) % 4) for z in range(4) for y in range(4)
    ]
    return lax.ppermute(value, "replica", pairs)


def pack_kernel(tokens_ref, weights_ref, packed_ref, *refs):
    share_refs, columns_ref, rows_ref, sems = refs[:4], refs[4], refs[5], refs[6]
    slab = lax.axis_index("fsdp") // PLANE
    y = lax.rem(lax.axis_index("replica"), 4)
    width = packed_ref.shape[2] // SLABS
    loads = []
    for k, step in enumerate((0, 3, 1, 2)):
        start = pl.multiple_of(lax.rem(slab + step, SLABS) * (PLANE * width), PLANE * width)
        loads.append(
            pltpu.make_async_copy(
                tokens_ref.at[:, pl.ds(start, PLANE * width)], columns_ref.at[k], sems.at[k]
            )
        )
    loads.append(pltpu.make_async_copy(weights_ref, rows_ref, sems.at[SLABS]))
    for load in loads:
        load.start()
    stores = []
    for k in range(SLABS):
        loads[k].wait()
        for i in range(PLANE):
            stores.append(
                pltpu.make_async_copy(
                    columns_ref.at[k, :, pl.ds(i * width, width)],
                    packed_ref.at[i, :, pl.ds(k * width, width)],
                    sems.at[SLABS + 1],
                )
            )
            stores[-1].start()
    loads[SLABS].wait()
    for step, share_ref in enumerate(share_refs):
        stores.append(
            pltpu.make_async_copy(
                rows_ref.at[:, lax.rem(y + step, 4)], share_ref, sems.at[SLABS + 1]
            )
        )
        stores[-1].start()
    for store in stores:
        store.wait()


def pack(tokens, weights):
    rows, width = tokens.shape[0], weights.shape[0]
    weights = weights.reshape(4, 4, width // 16, weights.shape[1])
    share = jax.ShapeDtypeStruct((4,) + weights.shape[2:], weights.dtype)
    packed, *shares = pl.pallas_call(
        pack_kernel,
        out_shape=[
            jax.ShapeDtypeStruct((PLANE, rows, SLABS * width), tokens.dtype),
            *[share] * 4,
        ],
        in_specs=[pl.BlockSpec(memory_space=pltpu.HBM)] * 2,
        out_specs=[pl.BlockSpec(memory_space=pltpu.HBM)] * 5,
        scratch_shapes=[
            pltpu.VMEM((SLABS, rows, PLANE * width), tokens.dtype),
            pltpu.VMEM(weights.shape, weights.dtype),
            pltpu.SemaphoreType.DMA((SLABS + 2,)),
        ],
        compiler_params=pltpu.CompilerParams(vmem_limit_bytes=16 << 20),
        name="pack_columns",
    )(tokens, weights)
    return packed, shares


def add_kernel(*refs):
    z = lax.axis_index("replica") // 4
    for step in range(4):
        at = lax.rem(z + step, 4)
        total = refs[0][at].astype(jnp.float32)
        for ref in refs[1:4]:
            total += ref[at].astype(jnp.float32)
        refs[4 + step][...] = total


def add_shares(shares):
    return pl.pallas_call(
        add_kernel,
        out_shape=[jax.ShapeDtypeStruct(shares[0].shape[1:], jnp.float32)] * 4,
        name="add_shares",
    )(*shares)


def place_kernel(*refs):
    z, y = lax.axis_index("replica") // 4, lax.rem(lax.axis_index("replica"), 4)
    out_ref = refs[4]
    rows = refs[0].shape[1]
    for y_step in range(4):
        for z_step in range(4):
            at = lax.rem(z + 4 - z_step, 4) * 4 + lax.rem(y + 4 - y_step, 4)
            out_ref[pl.ds(pl.multiple_of(at * rows, rows), rows), :] = refs[y_step][z_step]


def place_shares(shares):
    _, rows, out_width = shares[0].shape
    return pl.pallas_call(
        place_kernel,
        out_shape=jax.ShapeDtypeStruct((16 * rows, out_width), shares[0].dtype),
        name="place_shares",
    )(*shares)


def project_kernel(x_ref, w0_ref, w1_ref, w2_ref, w3_ref, *out_refs):
    width = w0_ref.shape[0]
    part_width = out_refs[0].shape[2]
    for h, out_ref in enumerate(out_refs):
        total = None
        for k, w_ref in enumerate((w0_ref, w1_ref, w2_ref, w3_ref)):
            part = jnp.dot(
                x_ref[:, k * width : (k + 1) * width],
                w_ref[:, h * part_width : (h + 1) * part_width],
                preferred_element_type=jnp.float32,
            )
            total = part if total is None else total + part
        out_ref[...] = total.astype(out_ref.dtype).reshape(out_ref.shape)


def project(columns, pieces):
    shape = (PLANE, columns.shape[0] // PLANE, pieces[0].shape[1] // PARTS)
    return pl.pallas_call(
        project_kernel,
        out_shape=[jax.ShapeDtypeStruct(shape, jnp.bfloat16)] * PARTS,
        compiler_params=pltpu.CompilerParams(vmem_limit_bytes=32 << 20),
        name="project",
    )(columns, *pieces)


def gradient_kernel(slabs, columns_ref, rows_ref, *out_refs):
    width, part_width = out_refs[0].shape
    rows = rows_ref[:, :, :part_width].reshape(columns_ref.shape[0], part_width)
    for k, out_ref in zip(slabs, out_refs):
        total = lax.dot_general(
            columns_ref[:, k * width : (k + 1) * width],
            rows,
            (((0,), (0,)), ((), ())),
            preferred_element_type=jnp.float32,
        )
        out_ref[...] = total.astype(out_ref.dtype)


def gradient_of(columns, residuals, slabs, width, part_width, dtype):
    return pl.pallas_call(
        functools.partial(gradient_kernel, slabs),
        out_shape=[jax.ShapeDtypeStruct((width, part_width), dtype)] * len(slabs),
        compiler_params=pltpu.CompilerParams(vmem_limit_bytes=32 << 20),
        name="gradient",
    )(columns, residuals)


def to_plane(value):
    return lax.all_to_all(value, "fsdp", 0, 0, axis_index_groups=PLANES)


def scatter_z(blocks):
    own, to_before, to_after, far = blocks
    half = own.shape[0] // 2
    passing_up = shift_z(far[:half], 1).astype(jnp.float32)
    passing_down = shift_z(far[half:], -1).astype(jnp.float32)
    up = jnp.concatenate([to_after[:half] + passing_up, to_after[half:]], axis=0)
    down = jnp.concatenate([to_before[:half], to_before[half:] + passing_down], axis=0)
    from_before = shift_z(up.astype(jnp.bfloat16), 1)
    from_after = shift_z(down.astype(jnp.bfloat16), -1)
    return own + (from_before.astype(jnp.float32) + from_after.astype(jnp.float32))


def shards(weights, first_moment, second_moment, anchor, momentum, inputs, targets, keep_mask):
    initial = weights[0]
    tokens = inputs[0]
    goal_rows = targets[0]
    mask_rows = keep_mask[0].astype(jnp.float32)[:, None]
    rows = tokens.shape[0]
    width, out_width = initial.shape
    token_count = rows * lax.axis_size("fsdp")
    workers = lax.axis_size("replica")
    half = width // 2

    packed, shares = pack(tokens, initial)
    columns = to_plane(packed).reshape(PLANE * rows, SLABS * width)
    shares[1:] = [shift_replica(shares[i], 0, i) for i in (1, 2, 3)]
    sums = add_shares(shares)

    before, after = shift_z(initial, 1), shift_z(initial, -1)
    before, after, *sums = lax.optimization_barrier((before, after, *sums))
    opposite = jnp.concatenate(
        [shift_z(before[:half], 1), shift_z(after[half:], -1)], axis=0
    )
    partials = list(project(columns, (initial, before, after, opposite)))

    partials[0], *sums = lax.optimization_barrier((partials[0], *sums))
    sums[1:] = [shift_replica(sums[i], i, 0) for i in (1, 2, 3)]
    weight_mean = (sums[0] + sums[1] + sums[2] + sums[3]) / workers
    pseudo_grad = anchor - weight_mean
    new_momentum = NESTEROV * momentum + pseudo_grad
    new_anchor = anchor - OUTER_RATE * (pseudo_grad + NESTEROV * new_momentum)

    part_width = out_width // PARTS

    def residual_of(mine, h):
        goal = goal_rows[:, h * part_width : (h + 1) * part_width].astype(jnp.float32)
        projected = jnp.sum(mine.astype(jnp.float32), 0)
        residual = ((projected - goal) * mask_rows / token_count).astype(jnp.bfloat16)
        return jnp.broadcast_to(residual[None], mine.shape)

    received = to_plane(partials[0])
    gradient = []
    for h in range(PARTS):
        out = residual_of(received[:, :, -part_width:], h)
        if h + 1 < PARTS:
            out = jnp.concatenate([out, partials[h + 1]], axis=2)
        if h == 0:
            out, shared = lax.optimization_barrier((out, new_anchor))
            shared = [shared] + [shift_replica(shared, i, 0) for i in (1, 2, 3)]
        received = to_plane(out)
        if h == 0:
            received, *shared = lax.optimization_barrier((received, *shared))
        (far,) = gradient_of(columns, received, (3,), width, part_width, jnp.bfloat16)
        near = gradient_of(columns, received, (0, 1, 2), width, part_width, jnp.float32)
        gradient.append(scatter_z((*near, far)))
    gradient = jnp.concatenate(gradient, axis=1)
    shared = jnp.stack(shared)
    block_anchor = place_shares(
        [shared] + [shift_replica(shared, 0, i) for i in (1, 2, 3)]
    )

    weight_f = initial.astype(jnp.float32)
    first_new = BETA_FIRST * first_moment[0] + (1.0 - BETA_FIRST) * gradient
    second_new = BETA_SECOND * second_moment[0] + (1.0 - BETA_SECOND) * gradient * gradient
    moved = weight_f - INNER_RATE * (
        first_new / (jnp.sqrt(second_new) + EPSILON) + WEIGHT_DECAY * weight_f
    )
    inner_weight = moved.astype(jnp.bfloat16)
    mixed = ((1.0 - MIXING) * block_anchor + MIXING * inner_weight.astype(jnp.float32)).astype(
        jnp.bfloat16
    )
    return (mixed[None], first_new[None], new_anchor, new_momentum)


def solution(mesh):
    return jax.shard_map(
        shards,
        mesh=mesh,
        in_specs=(
            P("replica", "fsdp", None),
            P("replica", "fsdp", None),
            P("replica", "fsdp", None),
            P(("fsdp", "replica"), None),
            P(("fsdp", "replica"), None),
            P("replica", "fsdp", None),
            P("replica", "fsdp", None),
            P("replica", "fsdp"),
        ),
        out_specs=(
            P("replica", "fsdp", None),
            P("replica", "fsdp", None),
            P(("fsdp", "replica"), None),
            P(("fsdp", "replica"), None),
        ),
        check_vma=False,
    )
```

```python
import functools

import jax
import jax.numpy as jnp
from jax import lax
from jax.experimental import pallas as pl
from jax.experimental.pallas import tpu as pltpu
from jax.sharding import PartitionSpec as P

BETA_FIRST = 0.9
BETA_SECOND = 0.95
EPSILON = 1e-08
INNER_RATE = 0.002
WEIGHT_DECAY = 0.1
OUTER_RATE = 0.7
NESTEROV = 0.9
MIXING = 0.5

SLABS = 4
PLANE = 8
PARTS = 1
PLANES = [[z * PLANE + i for i in range(PLANE)] for z in range(SLABS)]


def shift_ring(value, step):
    pairs = []
    for z in range(SLABS):
        for i in range(PLANE):
            to = z + step if i % 2 == 0 else z - step
            pairs.append((z * PLANE + i, to % SLABS * PLANE + i))
    return lax.ppermute(value, "fsdp", pairs)


def shift_replica(value, z_step, y_step):
    pairs = [
        (z * 4 + y, (z + z_step) % 4 * 4 + (y + y_step) % 4) for z in range(4) for y in range(4)
    ]
    return lax.ppermute(value, "replica", pairs)


def pack_kernel(tokens_ref, weights_ref, packed_ref, *refs):
    share_refs, columns_ref, rows_ref, sems = refs[:4], refs[4], refs[5], refs[6]
    slab = lax.axis_index("fsdp") // PLANE
    y = lax.rem(lax.axis_index("replica"), 4)
    width = packed_ref.shape[2] // SLABS
    loads = []
    for k, step in enumerate((0, 3, 1, 2)):
        start = pl.multiple_of(lax.rem(slab + step, SLABS) * (PLANE * width), PLANE * width)
        loads.append(
            pltpu.make_async_copy(
                tokens_ref.at[:, pl.ds(start, PLANE * width)], columns_ref.at[k], sems.at[k]
            )
        )
    loads.append(pltpu.make_async_copy(weights_ref, rows_ref, sems.at[SLABS]))
    for load in loads:
        load.start()
    stores = []
    for k in range(SLABS):
        loads[k].wait()
        for i in range(PLANE):
            place = (k, (0, 2, 1, 3)[k])[i % 2]
            stores.append(
                pltpu.make_async_copy(
                    columns_ref.at[k, :, pl.ds(i * width, width)],
                    packed_ref.at[i, :, pl.ds(place * width, width)],
                    sems.at[SLABS + 1],
                )
            )
            stores[-1].start()
    loads[SLABS].wait()
    for step, share_ref in enumerate(share_refs):
        stores.append(
            pltpu.make_async_copy(
                rows_ref.at[:, lax.rem(y + step, 4)], share_ref, sems.at[SLABS + 1]
            )
        )
        stores[-1].start()
    for store in stores:
        store.wait()


def pack(tokens, weights):
    rows, width = tokens.shape[0], weights.shape[0]
    weights = weights.reshape(4, 4, width // 16, weights.shape[1])
    share = jax.ShapeDtypeStruct((4,) + weights.shape[2:], weights.dtype)
    packed, *shares = pl.pallas_call(
        pack_kernel,
        out_shape=[
            jax.ShapeDtypeStruct((PLANE, rows, SLABS * width), tokens.dtype),
            *[share] * 4,
        ],
        in_specs=[pl.BlockSpec(memory_space=pltpu.HBM)] * 2,
        out_specs=[pl.BlockSpec(memory_space=pltpu.HBM)] * 5,
        scratch_shapes=[
            pltpu.VMEM((SLABS, rows, PLANE * width), tokens.dtype),
            pltpu.VMEM(weights.shape, weights.dtype),
            pltpu.SemaphoreType.DMA((SLABS + 2,)),
        ],
        compiler_params=pltpu.CompilerParams(vmem_limit_bytes=16 << 20),
        name="pack_columns",
    )(tokens, weights)
    return packed, shares


def add_kernel(*refs):
    z = lax.axis_index("replica") // 4
    for step in range(4):
        at = lax.rem(z + step, 4)
        total = refs[0][at].astype(jnp.float32)
        for ref in refs[1:4]:
            total += ref[at].astype(jnp.float32)
        refs[4 + step][...] = total


def add_shares(shares):
    return pl.pallas_call(
        add_kernel,
        out_shape=[jax.ShapeDtypeStruct(shares[0].shape[1:], jnp.float32)] * 4,
        name="add_shares",
    )(*shares)


def place_kernel(*refs):
    z, y = lax.axis_index("replica") // 4, lax.rem(lax.axis_index("replica"), 4)
    out_ref = refs[4]
    rows = refs[0].shape[1]
    for y_step in range(4):
        for z_step in range(4):
            at = lax.rem(z + 4 - z_step, 4) * 4 + lax.rem(y + 4 - y_step, 4)
            out_ref[pl.ds(pl.multiple_of(at * rows, rows), rows), :] = refs[y_step][z_step]


def place_shares(shares):
    _, rows, out_width = shares[0].shape
    return pl.pallas_call(
        place_kernel,
        out_shape=jax.ShapeDtypeStruct((16 * rows, out_width), shares[0].dtype),
        name="place_shares",
    )(*shares)


def project_kernel(x_ref, w0_ref, w1_ref, w2_ref, w3_ref, *out_refs):
    width = w0_ref.shape[0]
    part_width = out_refs[0].shape[2]
    for h, out_ref in enumerate(out_refs):
        total = None
        for k, w_ref in enumerate((w0_ref, w1_ref, w2_ref, w3_ref)):
            part = jnp.dot(
                x_ref[:, k * width : (k + 1) * width],
                w_ref[:, h * part_width : (h + 1) * part_width],
                preferred_element_type=jnp.float32,
            )
            total = part if total is None else total + part
        out_ref[...] = total.astype(out_ref.dtype).reshape(out_ref.shape)


def project(columns, pieces):
    shape = (PLANE, columns.shape[0] // PLANE, pieces[0].shape[1] // PARTS)
    return pl.pallas_call(
        project_kernel,
        out_shape=[jax.ShapeDtypeStruct(shape, jnp.bfloat16)] * PARTS,
        compiler_params=pltpu.CompilerParams(vmem_limit_bytes=32 << 20),
        name="project",
    )(columns, *pieces)


def gradient_kernel(slabs, columns_ref, rows_ref, *out_refs):
    width, part_width = out_refs[0].shape
    rows = rows_ref[:, :, :part_width].reshape(columns_ref.shape[0], part_width)
    for k, out_ref in zip(slabs, out_refs):
        total = lax.dot_general(
            columns_ref[:, k * width : (k + 1) * width],
            rows,
            (((0,), (0,)), ((), ())),
            preferred_element_type=jnp.float32,
        )
        out_ref[...] = total.astype(out_ref.dtype)


def gradient_of(columns, residuals, slabs, width, part_width, dtype):
    return pl.pallas_call(
        functools.partial(gradient_kernel, slabs),
        out_shape=[jax.ShapeDtypeStruct((width, part_width), dtype)] * len(slabs),
        compiler_params=pltpu.CompilerParams(vmem_limit_bytes=32 << 20),
        name="gradient",
    )(columns, residuals)


def to_plane(value):
    return lax.all_to_all(value, "fsdp", 0, 0, axis_index_groups=PLANES)


def scatter_ring(blocks, beside):
    own, to_previous, to_next, far = blocks
    passing = shift_ring(far, 1)
    passing, *beside = lax.optimization_barrier((passing, *beside))
    from_next = shift_ring(to_previous.astype(jnp.bfloat16), -1)
    both = (to_next + passing.astype(jnp.float32)).astype(jnp.bfloat16)
    from_previous = shift_ring(both, 1)
    total = own + (from_previous.astype(jnp.float32) + from_next.astype(jnp.float32))
    return total, beside


def shards(weights, first_moment, second_moment, anchor, momentum, inputs, targets, keep_mask):
    initial = weights[0]
    tokens = inputs[0]
    goal_rows = targets[0]
    mask_rows = keep_mask[0].astype(jnp.float32)[:, None]
    rows = tokens.shape[0]
    width, out_width = initial.shape
    token_count = rows * lax.axis_size("fsdp")
    workers = lax.axis_size("replica")

    packed, shares = pack(tokens, initial)
    columns = to_plane(packed).reshape(PLANE * rows, SLABS * width)
    shares[1:] = [shift_replica(shares[i], 0, i) for i in (1, 2, 3)]
    sums = add_shares(shares)

    previous, following = shift_ring(initial, 1), shift_ring(initial, -1)
    previous, *sums = lax.optimization_barrier((previous, *sums))
    opposite = shift_ring(previous, 1)
    partials = list(project(columns, (initial, previous, following, opposite)))

    partials[0], *sums = lax.optimization_barrier((partials[0], *sums))
    sums[1:] = [shift_replica(sums[i], i, 0) for i in (1, 2, 3)]
    weight_mean = (sums[0] + sums[1] + sums[2] + sums[3]) / workers
    pseudo_grad = anchor - weight_mean
    new_momentum = NESTEROV * momentum + pseudo_grad
    new_anchor = anchor - OUTER_RATE * (pseudo_grad + NESTEROV * new_momentum)

    part_width = out_width // PARTS

    def residual_of(mine, h):
        goal = goal_rows[:, h * part_width : (h + 1) * part_width].astype(jnp.float32)
        projected = jnp.sum(mine.astype(jnp.float32), 0)
        residual = ((projected - goal) * mask_rows / token_count).astype(jnp.bfloat16)
        return jnp.broadcast_to(residual[None], mine.shape)

    received = to_plane(partials[0])
    out = residual_of(received, 0)
    out, shared = lax.optimization_barrier((out, new_anchor))
    shared = [shared] + [shift_replica(shared, i, 0) for i in (1, 2, 3)]
    received = to_plane(out)
    received, *shared = lax.optimization_barrier((received, *shared))
    (far,) = gradient_of(columns, received, (3,), width, part_width, jnp.bfloat16)
    near = gradient_of(columns, received, (0, 1, 2), width, part_width, jnp.float32)
    shared = jnp.stack(shared)
    shared = [shared] + [shift_replica(shared, 0, i) for i in (1, 2, 3)]
    gradient, shared = scatter_ring((*near, far), shared)
    block_anchor = place_shares(shared)

    weight_f = initial.astype(jnp.float32)
    first_new = BETA_FIRST * first_moment[0] + (1.0 - BETA_FIRST) * gradient
    second_new = BETA_SECOND * second_moment[0] + (1.0 - BETA_SECOND) * gradient * gradient
    moved = weight_f - INNER_RATE * (
        first_new / (jnp.sqrt(second_new) + EPSILON) + WEIGHT_DECAY * weight_f
    )
    inner_weight = moved.astype(jnp.bfloat16)
    mixed = ((1.0 - MIXING) * block_anchor + MIXING * inner_weight.astype(jnp.float32)).astype(
        jnp.bfloat16
    )
    return (mixed[None], first_new[None], new_anchor, new_momentum)


def solution(mesh):
    return jax.shard_map(
        shards,
        mesh=mesh,
        in_specs=(
            P("replica", "fsdp", None),
            P("replica", "fsdp", None),
            P("replica", "fsdp", None),
            P(("fsdp", "replica"), None),
            P(("fsdp", "replica"), None),
            P("replica", "fsdp", None),
            P("replica", "fsdp", None),
            P("replica", "fsdp"),
        ),
        out_specs=(
            P("replica", "fsdp", None),
            P("replica", "fsdp", None),
            P(("fsdp", "replica"), None),
            P(("fsdp", "replica"), None),
        ),
        check_vma=False,
    )
```

```python
import functools

import jax
import jax.numpy as jnp
from jax import lax
from jax.experimental import pallas as pl
from jax.experimental.pallas import tpu as pltpu
from jax.sharding import PartitionSpec as P

BETA_FIRST = 0.9
BETA_SECOND = 0.95
EPSILON = 1e-08
INNER_RATE = 0.002
WEIGHT_DECAY = 0.1
OUTER_RATE = 0.7
NESTEROV = 0.9
MIXING = 0.5

SLABS = 4
PLANE = 8
PARTS = 1
PLANES = [[z * PLANE + i for i in range(PLANE)] for z in range(SLABS)]


def shift_ring(value, step):
    pairs = []
    for z in range(SLABS):
        for i in range(PLANE):
            to = z + step if i % 2 == 0 else z - step
            pairs.append((z * PLANE + i, to % SLABS * PLANE + i))
    return lax.ppermute(value, "fsdp", pairs)


def shift_replica(value, z_step, y_step):
    pairs = [
        (z * 4 + y, (z + z_step) % 4 * 4 + (y + y_step) % 4) for z in range(4) for y in range(4)
    ]
    return lax.ppermute(value, "replica", pairs)


def pack_kernel(tokens_ref, weights_ref, packed_ref, *refs):
    share_refs, columns_ref, rows_ref, sems = refs[:4], refs[4], refs[5], refs[6]
    slab = lax.axis_index("fsdp") // PLANE
    y = lax.rem(lax.axis_index("replica"), 4)
    width = packed_ref.shape[2] // SLABS
    loads = []
    for k, step in enumerate((0, 3, 1, 2)):
        start = pl.multiple_of(lax.rem(slab + step, SLABS) * (PLANE * width), PLANE * width)
        loads.append(
            pltpu.make_async_copy(
                tokens_ref.at[:, pl.ds(start, PLANE * width)], columns_ref.at[k], sems.at[k]
            )
        )
    loads.append(pltpu.make_async_copy(weights_ref, rows_ref, sems.at[SLABS]))
    for load in loads:
        load.start()
    stores = []
    for k in range(SLABS):
        loads[k].wait()
        for i in range(PLANE):
            place = (k, (0, 2, 1, 3)[k])[i % 2]
            stores.append(
                pltpu.make_async_copy(
                    columns_ref.at[k, :, pl.ds(i * width, width)],
                    packed_ref.at[i, :, pl.ds(place * width, width)],
                    sems.at[SLABS + 1],
                )
            )
            stores[-1].start()
    loads[SLABS].wait()
    for step, share_ref in enumerate(share_refs):
        stores.append(
            pltpu.make_async_copy(
                rows_ref.at[:, lax.rem(y + step, 4)], share_ref, sems.at[SLABS + 1]
            )
        )
        stores[-1].start()
    for store in stores:
        store.wait()


def pack(tokens, weights):
    rows, width = tokens.shape[0], weights.shape[0]
    weights = weights.reshape(4, 4, width // 16, weights.shape[1])
    share = jax.ShapeDtypeStruct((4,) + weights.shape[2:], weights.dtype)
    packed, *shares = pl.pallas_call(
        pack_kernel,
        out_shape=[
            jax.ShapeDtypeStruct((PLANE, rows, SLABS * width), tokens.dtype),
            *[share] * 4,
        ],
        in_specs=[pl.BlockSpec(memory_space=pltpu.HBM)] * 2,
        out_specs=[pl.BlockSpec(memory_space=pltpu.HBM)] * 5,
        scratch_shapes=[
            pltpu.VMEM((SLABS, rows, PLANE * width), tokens.dtype),
            pltpu.VMEM(weights.shape, weights.dtype),
            pltpu.SemaphoreType.DMA((SLABS + 2,)),
        ],
        compiler_params=pltpu.CompilerParams(vmem_limit_bytes=16 << 20),
        name="pack_columns",
    )(tokens, weights)
    return packed, shares


def add_kernel(*refs):
    z = lax.axis_index("replica") // 4
    for step in range(4):
        at = lax.rem(z + step, 4)
        total = refs[0][at].astype(jnp.float32)
        for ref in refs[1:4]:
            total += ref[at].astype(jnp.float32)
        refs[4 + step][...] = total


def add_shares(shares):
    return pl.pallas_call(
        add_kernel,
        out_shape=[jax.ShapeDtypeStruct(shares[0].shape[1:], jnp.float32)] * 4,
        name="add_shares",
    )(*shares)


def place_kernel(*refs):
    z, y = lax.axis_index("replica") // 4, lax.rem(lax.axis_index("replica"), 4)
    out_ref = refs[4]
    rows = refs[0].shape[1]
    for y_step in range(4):
        for z_step in range(4):
            at = lax.rem(z + 4 - z_step, 4) * 4 + lax.rem(y + 4 - y_step, 4)
            out_ref[pl.ds(pl.multiple_of(at * rows, rows), rows), :] = refs[y_step][z_step]


def place_shares(shares):
    _, rows, out_width = shares[0].shape
    return pl.pallas_call(
        place_kernel,
        out_shape=jax.ShapeDtypeStruct((16 * rows, out_width), shares[0].dtype),
        name="place_shares",
    )(*shares)


def mask_kernel(keep_ref, mask_ref):
    mask_ref[...] = keep_ref[...].astype(mask_ref.dtype)


def mask_of(keep):
    return pl.pallas_call(
        mask_kernel,
        out_shape=jax.ShapeDtypeStruct(keep.shape, jnp.float32),
        cost_estimate=pl.CostEstimate(flops=20 * 10**9, bytes_accessed=1 << 10, transcendentals=0),
        name="mask",
    )(keep)


def project_kernel(x_ref, w0_ref, w1_ref, w2_ref, w3_ref, *out_refs):
    width = w0_ref.shape[0]
    part_width = out_refs[0].shape[2]
    for h, out_ref in enumerate(out_refs):
        total = None
        for k, w_ref in enumerate((w0_ref, w1_ref, w2_ref, w3_ref)):
            part = jnp.dot(
                x_ref[:, k * width : (k + 1) * width],
                w_ref[:, h * part_width : (h + 1) * part_width],
                preferred_element_type=jnp.float32,
            )
            total = part if total is None else total + part
        out_ref[...] = total.astype(out_ref.dtype).reshape(out_ref.shape)


def project(columns, pieces):
    shape = (PLANE, columns.shape[0] // PLANE, pieces[0].shape[1] // PARTS)
    return pl.pallas_call(
        project_kernel,
        out_shape=[jax.ShapeDtypeStruct(shape, jnp.bfloat16)] * PARTS,
        compiler_params=pltpu.CompilerParams(vmem_limit_bytes=32 << 20),
        name="project",
    )(columns, *pieces)


def gradient_kernel(slabs, columns_ref, rows_ref, *out_refs):
    width, part_width = out_refs[0].shape
    rows = rows_ref[:, :, :part_width].reshape(columns_ref.shape[0], part_width)
    for k, out_ref in zip(slabs, out_refs):
        total = lax.dot_general(
            columns_ref[:, k * width : (k + 1) * width],
            rows,
            (((0,), (0,)), ((), ())),
            preferred_element_type=jnp.float32,
        )
        out_ref[...] = total.astype(out_ref.dtype)


def gradient_of(columns, residuals, slabs, width, part_width, dtype):
    return pl.pallas_call(
        functools.partial(gradient_kernel, slabs),
        out_shape=[jax.ShapeDtypeStruct((width, part_width), dtype)] * len(slabs),
        compiler_params=pltpu.CompilerParams(vmem_limit_bytes=32 << 20),
        name="gradient",
    )(columns, residuals)


def to_plane(value):
    return lax.all_to_all(value, "fsdp", 0, 0, axis_index_groups=PLANES)


def scatter_ring(blocks, beside):
    own, to_previous, to_next, far = blocks
    passing = shift_ring(far, 1)
    passing, *beside = lax.optimization_barrier((passing, *beside))
    from_next = shift_ring(to_previous.astype(jnp.bfloat16), -1)
    both = (to_next + passing.astype(jnp.float32)).astype(jnp.bfloat16)
    from_previous = shift_ring(both, 1)
    total = own + (from_previous.astype(jnp.float32) + from_next.astype(jnp.float32))
    return total, beside


def shards(weights, first_moment, second_moment, anchor, momentum, inputs, targets, keep_mask):
    initial = weights[0]
    tokens = inputs[0]
    goal_rows = targets[0]
    mask = mask_of(keep_mask)
    rows = tokens.shape[0]
    width, out_width = initial.shape
    token_count = rows * lax.axis_size("fsdp")
    workers = lax.axis_size("replica")

    packed, shares = pack(tokens, initial)
    columns = to_plane(packed).reshape(PLANE * rows, SLABS * width)
    shares[1:] = [shift_replica(shares[i], 0, i) for i in (1, 2, 3)]
    sums = add_shares(shares)

    previous, following = shift_ring(initial, 1), shift_ring(initial, -1)
    previous, mask = lax.optimization_barrier((previous, mask))
    opposite = shift_ring(previous, 1)
    columns, *sums = lax.optimization_barrier((columns, *sums))
    partials = list(project(columns, (initial, previous, following, opposite)))

    partials[0], *sums = lax.optimization_barrier((partials[0], *sums))
    sums[1:] = [shift_replica(sums[i], i, 0) for i in (1, 2, 3)]
    weight_mean = (sums[0] + sums[1] + sums[2] + sums[3]) / workers
    pseudo_grad = anchor - weight_mean
    new_momentum = NESTEROV * momentum + pseudo_grad
    new_anchor = anchor - OUTER_RATE * (pseudo_grad + NESTEROV * new_momentum)

    part_width = out_width // PARTS

    def residual_of(mine, h):
        goal = goal_rows[:, h * part_width : (h + 1) * part_width].astype(jnp.float32)
        projected = jnp.sum(mine.astype(jnp.float32), 0)
        residual = ((projected - goal) * mask[0][:, None] / token_count).astype(jnp.bfloat16)
        return jnp.broadcast_to(residual[None], mine.shape)

    received = to_plane(partials[0])
    out = residual_of(received, 0)
    out, shared = lax.optimization_barrier((out, new_anchor))
    shared = [shared] + [shift_replica(shared, i, 0) for i in (1, 2, 3)]
    received = to_plane(out)
    received, *shared = lax.optimization_barrier((received, *shared))
    (far,) = gradient_of(columns, received, (3,), width, part_width, jnp.bfloat16)
    near = gradient_of(columns, received, (0, 1, 2), width, part_width, jnp.float32)
    shared = jnp.stack(shared)
    shared = [shared] + [shift_replica(shared, 0, i) for i in (1, 2, 3)]
    gradient, shared = scatter_ring((*near, far), shared)
    block_anchor = place_shares(shared)

    weight_f = initial.astype(jnp.float32)
    first_new = BETA_FIRST * first_moment[0] + (1.0 - BETA_FIRST) * gradient
    second_new = BETA_SECOND * second_moment[0] + (1.0 - BETA_SECOND) * gradient * gradient
    moved = weight_f - INNER_RATE * (
        first_new / (jnp.sqrt(second_new) + EPSILON) + WEIGHT_DECAY * weight_f
    )
    inner_weight = moved.astype(jnp.bfloat16)
    mixed = ((1.0 - MIXING) * block_anchor + MIXING * inner_weight.astype(jnp.float32)).astype(
        jnp.bfloat16
    )
    return (mixed[None], first_new[None], new_anchor, new_momentum)


def solution(mesh):
    return jax.shard_map(
        shards,
        mesh=mesh,
        in_specs=(
            P("replica", "fsdp", None),
            P("replica", "fsdp", None),
            P("replica", "fsdp", None),
            P(("fsdp", "replica"), None),
            P(("fsdp", "replica"), None),
            P("replica", "fsdp", None),
            P("replica", "fsdp", None),
            P("replica", "fsdp"),
        ),
        out_specs=(
            P("replica", "fsdp", None),
            P("replica", "fsdp", None),
            P(("fsdp", "replica"), None),
            P(("fsdp", "replica"), None),
        ),
        check_vma=False,
    )
```

```python
import functools

import jax
import jax.numpy as jnp
from jax import lax
from jax.experimental import pallas as pl
from jax.experimental.pallas import tpu as pltpu
from jax.sharding import PartitionSpec as P

BETA_FIRST = 0.9
BETA_SECOND = 0.95
EPSILON = 1e-08
INNER_RATE = 0.002
WEIGHT_DECAY = 0.1
OUTER_RATE = 0.7
NESTEROV = 0.9
MIXING = 0.5

SLABS = 4
PLANE = 8
PARTS = 1
PLANES = [[z * PLANE + i for i in range(PLANE)] for z in range(SLABS)]


def shift_ring(value, step):
    pairs = []
    for z in range(SLABS):
        for i in range(PLANE):
            to = z + step if i % 2 == 0 else z - step
            pairs.append((z * PLANE + i, to % SLABS * PLANE + i))
    return lax.ppermute(value, "fsdp", pairs)


def shift_replica(value, z_step, y_step):
    pairs = [
        (z * 4 + y, (z + z_step) % 4 * 4 + (y + y_step) % 4) for z in range(4) for y in range(4)
    ]
    return lax.ppermute(value, "replica", pairs)


def pack_kernel(tokens_ref, weights_ref, packed_ref, *refs):
    share_refs, columns_ref, rows_ref, sems = refs[:4], refs[4], refs[5], refs[6]
    slab = lax.axis_index("fsdp") // PLANE
    y = lax.rem(lax.axis_index("replica"), 4)
    width = packed_ref.shape[2] // SLABS
    loads = []
    for k, step in enumerate((0, 3, 1, 2)):
        start = pl.multiple_of(lax.rem(slab + step, SLABS) * (PLANE * width), PLANE * width)
        loads.append(
            pltpu.make_async_copy(
                tokens_ref.at[:, pl.ds(start, PLANE * width)], columns_ref.at[k], sems.at[k]
            )
        )
    loads.append(pltpu.make_async_copy(weights_ref, rows_ref, sems.at[SLABS]))
    for load in loads:
        load.start()
    stores = []
    for k in range(SLABS):
        loads[k].wait()
        for i in range(PLANE):
            place = (k, (0, 2, 1, 3)[k])[i % 2]
            stores.append(
                pltpu.make_async_copy(
                    columns_ref.at[k, :, pl.ds(i * width, width)],
                    packed_ref.at[i, :, pl.ds(place * width, width)],
                    sems.at[SLABS + 1],
                )
            )
            stores[-1].start()
    loads[SLABS].wait()
    for step, share_ref in enumerate(share_refs):
        stores.append(
            pltpu.make_async_copy(
                rows_ref.at[:, lax.rem(y + step, 4)], share_ref, sems.at[SLABS + 1]
            )
        )
        stores[-1].start()
    for store in stores:
        store.wait()


def pack(tokens, weights):
    rows, width = tokens.shape[0], weights.shape[0]
    weights = weights.reshape(4, 4, width // 16, weights.shape[1])
    share = jax.ShapeDtypeStruct((4,) + weights.shape[2:], weights.dtype)
    packed, *shares = pl.pallas_call(
        pack_kernel,
        out_shape=[
            jax.ShapeDtypeStruct((PLANE, rows, SLABS * width), tokens.dtype),
            *[share] * 4,
        ],
        in_specs=[pl.BlockSpec(memory_space=pltpu.HBM)] * 2,
        out_specs=[pl.BlockSpec(memory_space=pltpu.HBM)] * 5,
        scratch_shapes=[
            pltpu.VMEM((SLABS, rows, PLANE * width), tokens.dtype),
            pltpu.VMEM(weights.shape, weights.dtype),
            pltpu.SemaphoreType.DMA((SLABS + 2,)),
        ],
        compiler_params=pltpu.CompilerParams(vmem_limit_bytes=16 << 20),
        name="pack_columns",
    )(tokens, weights)
    return packed, shares


def add_kernel(*refs):
    z = lax.axis_index("replica") // 4
    for step in range(4):
        at = lax.rem(z + step, 4)
        total = refs[0][at].astype(jnp.float32)
        for ref in refs[1:4]:
            total += ref[at].astype(jnp.float32)
        refs[4 + step][...] = total


def add_shares(shares):
    return pl.pallas_call(
        add_kernel,
        out_shape=[jax.ShapeDtypeStruct(shares[0].shape[1:], jnp.float32)] * 4,
        name="add_shares",
    )(*shares)


def place_kernel(*refs):
    z, y = lax.axis_index("replica") // 4, lax.rem(lax.axis_index("replica"), 4)
    out_ref = refs[4]
    rows = refs[0].shape[1]
    for y_step in range(4):
        for z_step in range(4):
            at = lax.rem(z + 4 - z_step, 4) * 4 + lax.rem(y + 4 - y_step, 4)
            out_ref[pl.ds(pl.multiple_of(at * rows, rows), rows), :] = refs[y_step][z_step]


def place_shares(shares):
    _, rows, out_width = shares[0].shape
    return pl.pallas_call(
        place_kernel,
        out_shape=jax.ShapeDtypeStruct((16 * rows, out_width), shares[0].dtype),
        name="place_shares",
    )(*shares)


def mask_kernel(keep_ref, mask_ref):
    mask_ref[...] = keep_ref[...].astype(mask_ref.dtype)


def mask_of(keep):
    return pl.pallas_call(
        mask_kernel,
        out_shape=jax.ShapeDtypeStruct(keep.shape, jnp.float32),
        cost_estimate=pl.CostEstimate(flops=20 * 10**9, bytes_accessed=1 << 10, transcendentals=0),
        name="mask",
    )(keep)


def project_kernel(x_ref, w0_ref, w1_ref, w2_ref, w3_ref, *out_refs):
    width = w0_ref.shape[0]
    part_width = out_refs[0].shape[2]
    for h, out_ref in enumerate(out_refs):
        total = None
        for k, w_ref in enumerate((w0_ref, w1_ref, w2_ref, w3_ref)):
            part = jnp.dot(
                x_ref[:, k * width : (k + 1) * width],
                w_ref[:, h * part_width : (h + 1) * part_width],
                preferred_element_type=jnp.float32,
            )
            total = part if total is None else total + part
        out_ref[...] = total.astype(out_ref.dtype).reshape(out_ref.shape)


def project(columns, pieces):
    shape = (PLANE, columns.shape[0] // PLANE, pieces[0].shape[1] // PARTS)
    return pl.pallas_call(
        project_kernel,
        out_shape=[jax.ShapeDtypeStruct(shape, jnp.bfloat16)] * PARTS,
        compiler_params=pltpu.CompilerParams(vmem_limit_bytes=32 << 20),
        name="project",
    )(columns, *pieces)


def gradient_kernel(slabs, columns_ref, rows_ref, *out_refs):
    width, part_width = out_refs[0].shape
    rows = rows_ref[:, :, :part_width].reshape(columns_ref.shape[0], part_width)
    for k, out_ref in zip(slabs, out_refs):
        total = lax.dot_general(
            columns_ref[:, k * width : (k + 1) * width],
            rows,
            (((0,), (0,)), ((), ())),
            preferred_element_type=jnp.float32,
        )
        out_ref[...] = total.astype(out_ref.dtype)


def gradient_of(columns, residuals, slabs, width, part_width, dtype):
    return pl.pallas_call(
        functools.partial(gradient_kernel, slabs),
        out_shape=[jax.ShapeDtypeStruct((width, part_width), dtype)] * len(slabs),
        compiler_params=pltpu.CompilerParams(vmem_limit_bytes=32 << 20),
        name="gradient",
    )(columns, residuals)


def to_plane(value):
    return lax.all_to_all(value, "fsdp", 0, 0, axis_index_groups=PLANES)


def scatter_ring(blocks, beside):
    own, to_previous, to_next, far = blocks
    passing = shift_ring(far, 1)
    passing, *beside = lax.optimization_barrier((passing, *beside))
    from_next = shift_ring(to_previous.astype(jnp.bfloat16), -1)
    both = (to_next + passing.astype(jnp.float32)).astype(jnp.bfloat16)
    from_previous = shift_ring(both, 1)
    total = own + (from_previous.astype(jnp.float32) + from_next.astype(jnp.float32))
    return total, beside


def shards(weights, first_moment, second_moment, anchor, momentum, inputs, targets, keep_mask):
    initial = weights[0]
    tokens = inputs[0]
    goal_rows = targets[0]
    mask = mask_of(keep_mask)
    rows = tokens.shape[0]
    width, out_width = initial.shape
    token_count = rows * lax.axis_size("fsdp")
    workers = lax.axis_size("replica")

    packed, shares = pack(tokens, initial)
    columns = to_plane(packed).reshape(PLANE * rows, SLABS * width)
    shares[1:] = [shift_replica(shares[i], 0, i) for i in (1, 2, 3)]

    previous, following = shift_ring(initial, 1), shift_ring(initial, -1)
    previous, mask, *shares[1:3] = lax.optimization_barrier((previous, mask, *shares[1:3]))
    opposite = shift_ring(previous, 1)
    sums = add_shares(shares)
    columns, *sums = lax.optimization_barrier((columns, *sums))
    partials = list(project(columns, (initial, previous, following, opposite)))

    partials[0], *sums = lax.optimization_barrier((partials[0], *sums))
    sums[1:] = [shift_replica(sums[i], i, 0) for i in (1, 2, 3)]
    weight_mean = (sums[0] + sums[1] + sums[2] + sums[3]) / workers
    pseudo_grad = anchor - weight_mean
    new_momentum = NESTEROV * momentum + pseudo_grad
    new_anchor = anchor - OUTER_RATE * (pseudo_grad + NESTEROV * new_momentum)

    part_width = out_width // PARTS

    def residual_of(mine, h):
        goal = goal_rows[:, h * part_width : (h + 1) * part_width].astype(jnp.float32)
        projected = jnp.sum(mine.astype(jnp.float32), 0)
        residual = ((projected - goal) * mask[0][:, None] / token_count).astype(jnp.bfloat16)
        return jnp.broadcast_to(residual[None], mine.shape)

    received = to_plane(partials[0])
    out = residual_of(received, 0)
    out, shared = lax.optimization_barrier((out, new_anchor))
    shared = [shared] + [shift_replica(shared, i, 0) for i in (1, 2, 3)]
    received = to_plane(out)
    received, *shared = lax.optimization_barrier((received, *shared))
    (far,) = gradient_of(columns, received, (3,), width, part_width, jnp.bfloat16)
    near = gradient_of(columns, received, (0, 1, 2), width, part_width, jnp.float32)
    shared = jnp.stack(shared)
    shared = [shared] + [shift_replica(shared, 0, i) for i in (1, 2, 3)]
    gradient, shared[:3] = scatter_ring((*near, far), shared[:3])
    block_anchor = place_shares(shared)

    weight_f = initial.astype(jnp.float32)
    first_new = BETA_FIRST * first_moment[0] + (1.0 - BETA_FIRST) * gradient
    second_new = BETA_SECOND * second_moment[0] + (1.0 - BETA_SECOND) * gradient * gradient
    moved = weight_f - INNER_RATE * (
        first_new / (jnp.sqrt(second_new) + EPSILON) + WEIGHT_DECAY * weight_f
    )
    inner_weight = moved.astype(jnp.bfloat16)
    mixed = ((1.0 - MIXING) * block_anchor + MIXING * inner_weight.astype(jnp.float32)).astype(
        jnp.bfloat16
    )
    return (mixed[None], first_new[None], new_anchor, new_momentum)


def solution(mesh):
    return jax.shard_map(
        shards,
        mesh=mesh,
        in_specs=(
            P("replica", "fsdp", None),
            P("replica", "fsdp", None),
            P("replica", "fsdp", None),
            P(("fsdp", "replica"), None),
            P(("fsdp", "replica"), None),
            P("replica", "fsdp", None),
            P("replica", "fsdp", None),
            P("replica", "fsdp"),
        ),
        out_specs=(
            P("replica", "fsdp", None),
            P("replica", "fsdp", None),
            P(("fsdp", "replica"), None),
            P(("fsdp", "replica"), None),
        ),
        check_vma=False,
    )
```

```python
import functools

import jax
import jax.numpy as jnp
from jax import lax
from jax.experimental import pallas as pl
from jax.experimental.pallas import tpu as pltpu
from jax.sharding import PartitionSpec as P

BETA_FIRST = 0.9
BETA_SECOND = 0.95
EPSILON = 1e-08
INNER_RATE = 0.002
WEIGHT_DECAY = 0.1
OUTER_RATE = 0.7
NESTEROV = 0.9
MIXING = 0.5

SLABS = 4
PLANE = 8
PARTS = 1
PLANES = [[z * PLANE + i for i in range(PLANE)] for z in range(SLABS)]


def shift_ring(value, step):
    pairs = []
    for z in range(SLABS):
        for i in range(PLANE):
            to = z + step if i % 2 == 0 else z - step
            pairs.append((z * PLANE + i, to % SLABS * PLANE + i))
    return lax.ppermute(value, "fsdp", pairs)


def shift_replica(value, z_step, y_step):
    pairs = [
        (z * 4 + y, (z + z_step) % 4 * 4 + (y + y_step) % 4) for z in range(4) for y in range(4)
    ]
    return lax.ppermute(value, "replica", pairs)


def pack_kernel(tokens_ref, weights_ref, packed_ref, *refs):
    share_refs, columns_ref, rows_ref, sems = refs[:4], refs[4], refs[5], refs[6]
    slab = lax.axis_index("fsdp") // PLANE
    y = lax.rem(lax.axis_index("replica"), 4)
    width = packed_ref.shape[2] // SLABS
    loads = []
    for k, step in enumerate((0, 3, 1, 2)):
        start = pl.multiple_of(lax.rem(slab + step, SLABS) * (PLANE * width), PLANE * width)
        loads.append(
            pltpu.make_async_copy(
                tokens_ref.at[:, pl.ds(start, PLANE * width)], columns_ref.at[k], sems.at[k]
            )
        )
    loads.append(pltpu.make_async_copy(weights_ref, rows_ref, sems.at[SLABS]))
    for load in loads:
        load.start()
    stores = []
    for k in range(SLABS):
        loads[k].wait()
        for i in range(PLANE):
            place = (k, (0, 2, 1, 3)[k])[i % 2]
            stores.append(
                pltpu.make_async_copy(
                    columns_ref.at[k, :, pl.ds(i * width, width)],
                    packed_ref.at[i, :, pl.ds(place * width, width)],
                    sems.at[SLABS + 1],
                )
            )
            stores[-1].start()
    loads[SLABS].wait()
    for step, share_ref in enumerate(share_refs):
        stores.append(
            pltpu.make_async_copy(
                rows_ref.at[:, lax.rem(y + step, 4)], share_ref, sems.at[SLABS + 1]
            )
        )
        stores[-1].start()
    for store in stores:
        store.wait()


def pack(tokens, weights):
    rows, width = tokens.shape[0], weights.shape[0]
    weights = weights.reshape(4, 4, width // 16, weights.shape[1])
    share = jax.ShapeDtypeStruct((4,) + weights.shape[2:], weights.dtype)
    packed, *shares = pl.pallas_call(
        pack_kernel,
        out_shape=[
            pltpu.HBM((PLANE, rows, SLABS * width), tokens.dtype),
            *[share] * 4,
        ],
        in_specs=[pl.BlockSpec(memory_space=pltpu.HBM)] * 2,
        out_specs=[pl.BlockSpec(memory_space=pltpu.HBM)] * 5,
        scratch_shapes=[
            pltpu.VMEM((SLABS, rows, PLANE * width), tokens.dtype),
            pltpu.VMEM(weights.shape, weights.dtype),
            pltpu.SemaphoreType.DMA((SLABS + 2,)),
        ],
        compiler_params=pltpu.CompilerParams(vmem_limit_bytes=16 << 20),
        name="pack_columns",
    )(pltpu.with_memory_space_constraint(tokens, pltpu.HBM), weights)
    return packed, shares


def add_kernel(*refs):
    z = lax.axis_index("replica") // 4
    for step in range(4):
        at = lax.rem(z + step, 4)
        total = refs[0][at].astype(jnp.float32)
        for ref in refs[1:4]:
            total += ref[at].astype(jnp.float32)
        refs[4 + step][...] = total


def add_shares(shares):
    return pl.pallas_call(
        add_kernel,
        out_shape=[jax.ShapeDtypeStruct(shares[0].shape[1:], jnp.float32)] * 4,
        name="add_shares",
    )(*shares)


def place_kernel(*refs):
    z, y = lax.axis_index("replica") // 4, lax.rem(lax.axis_index("replica"), 4)
    out_ref = refs[4]
    rows = refs[0].shape[1]
    for y_step in range(4):
        for z_step in range(4):
            at = lax.rem(z + 4 - z_step, 4) * 4 + lax.rem(y + 4 - y_step, 4)
            out_ref[pl.ds(pl.multiple_of(at * rows, rows), rows), :] = refs[y_step][z_step]


def place_shares(shares):
    _, rows, out_width = shares[0].shape
    return pl.pallas_call(
        place_kernel,
        out_shape=jax.ShapeDtypeStruct((16 * rows, out_width), shares[0].dtype),
        name="place_shares",
    )(*shares)


def mask_kernel(keep_ref, mask_ref):
    mask_ref[...] = keep_ref[...].astype(mask_ref.dtype)


def mask_of(keep):
    return pl.pallas_call(
        mask_kernel,
        out_shape=jax.ShapeDtypeStruct(keep.shape, jnp.float32),
        cost_estimate=pl.CostEstimate(flops=20 * 10**9, bytes_accessed=1 << 10, transcendentals=0),
        name="mask",
    )(keep)


def project_kernel(x_ref, w0_ref, w1_ref, w2_ref, w3_ref, *out_refs):
    width = w0_ref.shape[0]
    part_width = out_refs[0].shape[2]
    for h, out_ref in enumerate(out_refs):
        total = None
        for k, w_ref in enumerate((w0_ref, w1_ref, w2_ref, w3_ref)):
            part = jnp.dot(
                x_ref[:, k * width : (k + 1) * width],
                w_ref[:, h * part_width : (h + 1) * part_width],
                preferred_element_type=jnp.float32,
            )
            total = part if total is None else total + part
        out_ref[...] = total.astype(out_ref.dtype).reshape(out_ref.shape)


def project(columns, pieces):
    shape = (PLANE, columns.shape[0] // PLANE, pieces[0].shape[1] // PARTS)
    return pl.pallas_call(
        project_kernel,
        out_shape=[jax.ShapeDtypeStruct(shape, jnp.bfloat16)] * PARTS,
        compiler_params=pltpu.CompilerParams(vmem_limit_bytes=32 << 20),
        name="project",
    )(columns, *pieces)


def gradient_kernel(slabs, columns_ref, rows_ref, *out_refs):
    width, part_width = out_refs[0].shape
    rows = rows_ref[:, :, :part_width].reshape(columns_ref.shape[0], part_width)
    for k, out_ref in zip(slabs, out_refs):
        total = lax.dot_general(
            columns_ref[:, k * width : (k + 1) * width],
            rows,
            (((0,), (0,)), ((), ())),
            preferred_element_type=jnp.float32,
        )
        out_ref[...] = total.astype(out_ref.dtype)


def gradient_of(columns, residuals, slabs, width, part_width, dtype):
    return pl.pallas_call(
        functools.partial(gradient_kernel, slabs),
        out_shape=[jax.ShapeDtypeStruct((width, part_width), dtype)] * len(slabs),
        compiler_params=pltpu.CompilerParams(vmem_limit_bytes=32 << 20),
        name="gradient",
    )(columns, residuals)


def to_plane(value):
    return lax.all_to_all(value, "fsdp", 0, 0, axis_index_groups=PLANES)


def scatter_ring(blocks, beside):
    own, to_previous, to_next, far = blocks
    passing = shift_ring(far, 1)
    passing, *beside = lax.optimization_barrier((passing, *beside))
    from_next = shift_ring(to_previous.astype(jnp.bfloat16), -1)
    both = (to_next + passing.astype(jnp.float32)).astype(jnp.bfloat16)
    from_previous = shift_ring(both, 1)
    total = own + (from_previous.astype(jnp.float32) + from_next.astype(jnp.float32))
    return total, beside


def shards(weights, first_moment, second_moment, anchor, momentum, inputs, targets, keep_mask):
    initial = weights[0]
    tokens = inputs[0]
    goal_rows = targets[0]
    mask = mask_of(keep_mask)
    rows = tokens.shape[0]
    width, out_width = initial.shape
    token_count = rows * lax.axis_size("fsdp")
    workers = lax.axis_size("replica")

    packed, shares = pack(tokens, initial)
    columns = to_plane(packed).reshape(PLANE * rows, SLABS * width)
    shares[1:] = [shift_replica(shares[i], 0, i) for i in (1, 2, 3)]

    previous, following = shift_ring(initial, 1), shift_ring(initial, -1)
    previous, mask, *shares[1:3] = lax.optimization_barrier((previous, mask, *shares[1:3]))
    opposite = shift_ring(previous, 1)
    sums = add_shares(shares)
    columns, *sums = lax.optimization_barrier((columns, *sums))
    partials = list(project(columns, (initial, previous, following, opposite)))

    partials[0], *sums = lax.optimization_barrier((partials[0], *sums))
    sums[1:] = [shift_replica(sums[i], i, 0) for i in (1, 2, 3)]
    part_width = out_width // PARTS

    def residual_of(mine, h):
        goal = goal_rows[:, h * part_width : (h + 1) * part_width].astype(jnp.float32)
        projected = jnp.sum(mine.astype(jnp.float32), 0)
        residual = ((projected - goal) * mask[0][:, None] / token_count).astype(jnp.bfloat16)
        return jnp.broadcast_to(residual[None], mine.shape)

    received = to_plane(partials[0])
    out = residual_of(received, 0)
    out, *sums = lax.optimization_barrier((out, *sums))
    weight_mean = (sums[0] + sums[1] + sums[2] + sums[3]) / workers
    pseudo_grad = anchor - weight_mean
    new_momentum = NESTEROV * momentum + pseudo_grad
    new_anchor = anchor - OUTER_RATE * (pseudo_grad + NESTEROV * new_momentum)
    shared = [new_anchor] + [shift_replica(new_anchor, i, 0) for i in (1, 2, 3)]
    received = to_plane(out)
    received, *shared = lax.optimization_barrier((received, *shared))
    (far,) = gradient_of(columns, received, (3,), width, part_width, jnp.bfloat16)
    near = gradient_of(columns, received, (0, 1, 2), width, part_width, jnp.float32)
    shared = jnp.stack(shared)
    shared = [shared] + [shift_replica(shared, 0, i) for i in (1, 2, 3)]
    gradient, shared[:3] = scatter_ring((*near, far), shared[:3])
    block_anchor = place_shares(shared)

    weight_f = initial.astype(jnp.float32)
    first_new = BETA_FIRST * first_moment[0] + (1.0 - BETA_FIRST) * gradient
    second_new = BETA_SECOND * second_moment[0] + (1.0 - BETA_SECOND) * gradient * gradient
    moved = weight_f - INNER_RATE * (
        first_new / (jnp.sqrt(second_new) + EPSILON) + WEIGHT_DECAY * weight_f
    )
    inner_weight = moved.astype(jnp.bfloat16)
    mixed = ((1.0 - MIXING) * block_anchor + MIXING * inner_weight.astype(jnp.float32)).astype(
        jnp.bfloat16
    )
    return (mixed[None], first_new[None], new_anchor, new_momentum)


def solution(mesh):
    return jax.shard_map(
        shards,
        mesh=mesh,
        in_specs=(
            P("replica", "fsdp", None),
            P("replica", "fsdp", None),
            P("replica", "fsdp", None),
            P(("fsdp", "replica"), None),
            P(("fsdp", "replica"), None),
            P("replica", "fsdp", None),
            P("replica", "fsdp", None),
            P("replica", "fsdp"),
        ),
        out_specs=(
            P("replica", "fsdp", None),
            P("replica", "fsdp", None),
            P(("fsdp", "replica"), None),
            P(("fsdp", "replica"), None),
        ),
        check_vma=False,
    )
```

```python
import functools

import jax
import jax.numpy as jnp
from jax import lax
from jax.experimental import pallas as pl
from jax.experimental.pallas import tpu as pltpu
from jax.sharding import PartitionSpec as P

BETA_FIRST = 0.9
BETA_SECOND = 0.95
EPSILON = 1e-08
INNER_RATE = 0.002
WEIGHT_DECAY = 0.1
OUTER_RATE = 0.7
NESTEROV = 0.9
MIXING = 0.5

SLABS = 4
PLANE = 8
PARTS = 1
PLANES = [[z * PLANE + i for i in range(PLANE)] for z in range(SLABS)]


def shift_ring(value, step):
    pairs = []
    for z in range(SLABS):
        for i in range(PLANE):
            to = z + step if i % 2 == 0 else z - step
            pairs.append((z * PLANE + i, to % SLABS * PLANE + i))
    return lax.ppermute(value, "fsdp", pairs)


def shift_replica(value, z_step, y_step):
    pairs = [
        (z * 4 + y, (z + z_step) % 4 * 4 + (y + y_step) % 4) for z in range(4) for y in range(4)
    ]
    return lax.ppermute(value, "replica", pairs)


def pack_kernel(tokens_ref, weights_ref, packed_ref, *refs):
    share_refs, columns_ref, rows_ref, sems = refs[:4], refs[4], refs[5], refs[6]
    slab = lax.axis_index("fsdp") // PLANE
    y = lax.rem(lax.axis_index("replica"), 4)
    width = packed_ref.shape[2] // SLABS
    loads = []
    for k, step in enumerate((0, 3, 1, 2)):
        start = pl.multiple_of(lax.rem(slab + step, SLABS) * (PLANE * width), PLANE * width)
        loads.append(
            pltpu.make_async_copy(
                tokens_ref.at[:, pl.ds(start, PLANE * width)], columns_ref.at[k], sems.at[k]
            )
        )
    loads.append(pltpu.make_async_copy(weights_ref, rows_ref, sems.at[SLABS]))
    for load in loads:
        load.start()
    stores = []
    for k in range(SLABS):
        loads[k].wait()
        for i in range(PLANE):
            place = (k, (0, 2, 1, 3)[k])[i % 2]
            stores.append(
                pltpu.make_async_copy(
                    columns_ref.at[k, :, pl.ds(i * width, width)],
                    packed_ref.at[i, :, pl.ds(place * width, width)],
                    sems.at[SLABS + 1],
                )
            )
            stores[-1].start()
    loads[SLABS].wait()
    for step, share_ref in enumerate(share_refs):
        stores.append(
            pltpu.make_async_copy(
                rows_ref.at[:, lax.rem(y + step, 4)], share_ref, sems.at[SLABS + 1]
            )
        )
        stores[-1].start()
    for store in stores:
        store.wait()


def pack(tokens, weights):
    rows, width = tokens.shape[0], weights.shape[0]
    weights = weights.reshape(4, 4, width // 16, weights.shape[1])
    share = jax.ShapeDtypeStruct((4,) + weights.shape[2:], weights.dtype)
    packed, *shares = pl.pallas_call(
        pack_kernel,
        out_shape=[
            pltpu.HBM((PLANE, rows, SLABS * width), tokens.dtype),
            *[share] * 4,
        ],
        in_specs=[pl.BlockSpec(memory_space=pltpu.HBM)] * 2,
        out_specs=[pl.BlockSpec(memory_space=pltpu.HBM)] * 5,
        scratch_shapes=[
            pltpu.VMEM((SLABS, rows, PLANE * width), tokens.dtype),
            pltpu.VMEM(weights.shape, weights.dtype),
            pltpu.SemaphoreType.DMA((SLABS + 2,)),
        ],
        compiler_params=pltpu.CompilerParams(vmem_limit_bytes=16 << 20),
        name="pack_columns",
    )(*[pltpu.with_memory_space_constraint(v, pltpu.HBM) for v in (tokens, weights)])
    return packed, shares


def add_kernel(*refs):
    z = lax.axis_index("replica") // 4
    for step in range(4):
        at = lax.rem(z + step, 4)
        total = refs[0][at].astype(jnp.float32)
        for ref in refs[1:4]:
            total += ref[at].astype(jnp.float32)
        refs[4 + step][...] = total


def add_shares(shares):
    return pl.pallas_call(
        add_kernel,
        out_shape=[jax.ShapeDtypeStruct(shares[0].shape[1:], jnp.float32)] * 4,
        name="add_shares",
    )(*[pltpu.with_memory_space_constraint(v, pltpu.VMEM) for v in shares])


def place_kernel(*refs):
    z, y = lax.axis_index("replica") // 4, lax.rem(lax.axis_index("replica"), 4)
    out_ref = refs[4]
    rows = refs[0].shape[1]
    for y_step in range(4):
        for z_step in range(4):
            at = lax.rem(z + 4 - z_step, 4) * 4 + lax.rem(y + 4 - y_step, 4)
            out_ref[pl.ds(pl.multiple_of(at * rows, rows), rows), :] = refs[y_step][z_step]


def place_shares(shares):
    _, rows, out_width = shares[0].shape
    return pl.pallas_call(
        place_kernel,
        out_shape=jax.ShapeDtypeStruct((16 * rows, out_width), shares[0].dtype),
        name="place_shares",
    )(*[pltpu.with_memory_space_constraint(v, pltpu.VMEM) for v in shares])


def mask_kernel(keep_ref, mask_ref):
    mask_ref[...] = keep_ref[...].astype(mask_ref.dtype)


def mask_of(keep):
    return pl.pallas_call(
        mask_kernel,
        out_shape=jax.ShapeDtypeStruct(keep.shape, jnp.float32),
        cost_estimate=pl.CostEstimate(flops=20 * 10**9, bytes_accessed=1 << 10, transcendentals=0),
        name="mask",
    )(keep)


def project_kernel(x_ref, w0_ref, w1_ref, w2_ref, w3_ref, *out_refs):
    width = w0_ref.shape[0]
    part_width = out_refs[0].shape[2]
    for h, out_ref in enumerate(out_refs):
        total = None
        for k, w_ref in enumerate((w0_ref, w1_ref, w2_ref, w3_ref)):
            part = jnp.dot(
                x_ref[:, k * width : (k + 1) * width],
                w_ref[:, h * part_width : (h + 1) * part_width],
                preferred_element_type=jnp.float32,
            )
            total = part if total is None else total + part
        out_ref[...] = total.astype(out_ref.dtype).reshape(out_ref.shape)


def project(columns, pieces):
    shape = (PLANE, columns.shape[0] // PLANE, pieces[0].shape[1] // PARTS)
    return pl.pallas_call(
        project_kernel,
        out_shape=[jax.ShapeDtypeStruct(shape, jnp.bfloat16)] * PARTS,
        compiler_params=pltpu.CompilerParams(vmem_limit_bytes=32 << 20),
        name="project",
    )(columns, *pieces)


def gradient_kernel(slabs, columns_ref, rows_ref, *out_refs):
    width, part_width = out_refs[0].shape
    rows = rows_ref[:, :, :part_width].reshape(columns_ref.shape[0], part_width)
    for k, out_ref in zip(slabs, out_refs):
        total = lax.dot_general(
            columns_ref[:, k * width : (k + 1) * width],
            rows,
            (((0,), (0,)), ((), ())),
            preferred_element_type=jnp.float32,
        )
        out_ref[...] = total.astype(out_ref.dtype)


def gradient_of(columns, residuals, slabs, width, part_width, dtype):
    return pl.pallas_call(
        functools.partial(gradient_kernel, slabs),
        out_shape=[jax.ShapeDtypeStruct((width, part_width), dtype)] * len(slabs),
        compiler_params=pltpu.CompilerParams(vmem_limit_bytes=32 << 20),
        name="gradient",
    )(columns, residuals)


def to_plane(value):
    return lax.all_to_all(value, "fsdp", 0, 0, axis_index_groups=PLANES)


def scatter_ring(blocks, beside):
    own, to_previous, to_next, far = blocks
    passing = shift_ring(far, 1)
    passing, *beside = lax.optimization_barrier((passing, *beside))
    from_next = shift_ring(to_previous.astype(jnp.bfloat16), -1)
    both = (to_next + passing.astype(jnp.float32)).astype(jnp.bfloat16)
    from_previous = shift_ring(both, 1)
    total = own + (from_previous.astype(jnp.float32) + from_next.astype(jnp.float32))
    return total, beside


def shards(weights, first_moment, second_moment, anchor, momentum, inputs, targets, keep_mask):
    initial = weights[0]
    tokens = inputs[0]
    goal_rows = targets[0]
    mask = mask_of(keep_mask)
    rows = tokens.shape[0]
    width, out_width = initial.shape
    token_count = rows * lax.axis_size("fsdp")
    workers = lax.axis_size("replica")

    packed, shares = pack(tokens, initial)
    columns = to_plane(packed).reshape(PLANE * rows, SLABS * width)
    shares[1:] = [shift_replica(shares[i], 0, i) for i in (1, 2, 3)]

    previous, following = shift_ring(initial, 1), shift_ring(initial, -1)
    previous, mask, *shares[1:2] = lax.optimization_barrier((previous, mask, *shares[1:2]))
    opposite = shift_ring(previous, 1)
    sums = add_shares(shares)
    columns, *sums = lax.optimization_barrier((columns, *sums))
    partials = list(project(columns, (initial, previous, following, opposite)))

    partials[0], *sums = lax.optimization_barrier((partials[0], *sums))
    sums[1:] = [shift_replica(sums[i], i, 0) for i in (1, 2, 3)]
    part_width = out_width // PARTS

    def residual_of(mine, h):
        goal = goal_rows[:, h * part_width : (h + 1) * part_width].astype(jnp.float32)
        projected = jnp.sum(mine.astype(jnp.float32), 0)
        residual = ((projected - goal) * mask[0][:, None] / token_count).astype(jnp.bfloat16)
        return jnp.broadcast_to(residual[None], mine.shape)

    received = to_plane(partials[0])
    out = residual_of(received, 0)
    out, *sums = lax.optimization_barrier((out, *sums))
    weight_mean = (sums[0] + sums[1] + sums[2] + sums[3]) / workers
    pseudo_grad = anchor - weight_mean
    new_momentum = NESTEROV * momentum + pseudo_grad
    new_anchor = anchor - OUTER_RATE * (pseudo_grad + NESTEROV * new_momentum)
    shared = [new_anchor] + [shift_replica(new_anchor, i, 0) for i in (1, 2, 3)]
    received = to_plane(out)
    received, *shared = lax.optimization_barrier((received, *shared))
    (far,) = gradient_of(columns, received, (3,), width, part_width, jnp.bfloat16)
    near = gradient_of(columns, received, (0, 1, 2), width, part_width, jnp.float32)
    shared = jnp.stack(shared)
    shared = [shared] + [shift_replica(shared, 0, i) for i in (1, 2, 3)]
    gradient, shared[:3] = scatter_ring((*near, far), shared[:3])
    block_anchor = place_shares(shared)

    weight_f = initial.astype(jnp.float32)
    first_new = BETA_FIRST * first_moment[0] + (1.0 - BETA_FIRST) * gradient
    second_new = BETA_SECOND * second_moment[0] + (1.0 - BETA_SECOND) * gradient * gradient
    moved = weight_f - INNER_RATE * (
        first_new / (jnp.sqrt(second_new) + EPSILON) + WEIGHT_DECAY * weight_f
    )
    inner_weight = moved.astype(jnp.bfloat16)
    mixed = ((1.0 - MIXING) * block_anchor + MIXING * inner_weight.astype(jnp.float32)).astype(
        jnp.bfloat16
    )
    return (mixed[None], first_new[None], new_anchor, new_momentum)


def solution(mesh):
    return jax.shard_map(
        shards,
        mesh=mesh,
        in_specs=(
            P("replica", "fsdp", None),
            P("replica", "fsdp", None),
            P("replica", "fsdp", None),
            P(("fsdp", "replica"), None),
            P(("fsdp", "replica"), None),
            P("replica", "fsdp", None),
            P("replica", "fsdp", None),
            P("replica", "fsdp"),
        ),
        out_specs=(
            P("replica", "fsdp", None),
            P("replica", "fsdp", None),
            P(("fsdp", "replica"), None),
            P(("fsdp", "replica"), None),
        ),
        check_vma=False,
    )
```

```python
import functools

import jax
import jax.numpy as jnp
from jax import lax
from jax.experimental import pallas as pl
from jax.experimental.pallas import tpu as pltpu
from jax.sharding import PartitionSpec as P

BETA_FIRST = 0.9
BETA_SECOND = 0.95
EPSILON = 1e-08
INNER_RATE = 0.002
WEIGHT_DECAY = 0.1
OUTER_RATE = 0.7
NESTEROV = 0.9
MIXING = 0.5

SLABS = 4
PLANE = 8
PARTS = 1
PLANES = [[z * PLANE + i for i in range(PLANE)] for z in range(SLABS)]


def shift_ring(value, step):
    pairs = []
    for z in range(SLABS):
        for i in range(PLANE):
            to = z + step if i % 2 == 0 else z - step
            pairs.append((z * PLANE + i, to % SLABS * PLANE + i))
    return lax.ppermute(value, "fsdp", pairs)


def shift_replica(value, z_step, y_step):
    pairs = [
        (z * 4 + y, (z + z_step) % 4 * 4 + (y + y_step) % 4) for z in range(4) for y in range(4)
    ]
    return lax.ppermute(value, "replica", pairs)


def pack_kernel(tokens_ref, weights_ref, packed_ref, *refs):
    share_refs, columns_ref, rows_ref, sems = refs[:4], refs[4], refs[5], refs[6]
    slab = lax.axis_index("fsdp") // PLANE
    y = lax.rem(lax.axis_index("replica"), 4)
    width = packed_ref.shape[2] // SLABS
    loads = []
    for k, step in enumerate((0, 3, 1, 2)):
        start = pl.multiple_of(lax.rem(slab + step, SLABS) * (PLANE * width), PLANE * width)
        loads.append(
            pltpu.make_async_copy(
                tokens_ref.at[:, pl.ds(start, PLANE * width)], columns_ref.at[k], sems.at[k]
            )
        )
    loads.append(pltpu.make_async_copy(weights_ref, rows_ref, sems.at[SLABS]))
    for load in loads:
        load.start()
    stores = []
    for k in range(SLABS):
        loads[k].wait()
        for i in range(PLANE):
            place = (k, (0, 2, 1, 3)[k])[i % 2]
            stores.append(
                pltpu.make_async_copy(
                    columns_ref.at[k, :, pl.ds(i * width, width)],
                    packed_ref.at[i, :, pl.ds(place * width, width)],
                    sems.at[SLABS + 1],
                )
            )
            stores[-1].start()
    loads[SLABS].wait()
    for step, share_ref in enumerate(share_refs):
        stores.append(
            pltpu.make_async_copy(
                rows_ref.at[:, lax.rem(y + step, 4)], share_ref, sems.at[SLABS + 1]
            )
        )
        stores[-1].start()
    for store in stores:
        store.wait()


def pack(tokens, weights):
    rows, width = tokens.shape[0], weights.shape[0]
    weights = weights.reshape(4, 4, width // 16, weights.shape[1])
    share = jax.ShapeDtypeStruct((4,) + weights.shape[2:], weights.dtype)
    packed, *shares = pl.pallas_call(
        pack_kernel,
        out_shape=[
            pltpu.HBM((PLANE, rows, SLABS * width), tokens.dtype),
            *[share] * 4,
        ],
        in_specs=[pl.BlockSpec(memory_space=pltpu.HBM)] * 2,
        out_specs=[pl.BlockSpec(memory_space=pltpu.HBM)] * 5,
        scratch_shapes=[
            pltpu.VMEM((SLABS, rows, PLANE * width), tokens.dtype),
            pltpu.VMEM(weights.shape, weights.dtype),
            pltpu.SemaphoreType.DMA((SLABS + 2,)),
        ],
        compiler_params=pltpu.CompilerParams(vmem_limit_bytes=16 << 20),
        name="pack_columns",
    )(*[pltpu.with_memory_space_constraint(v, pltpu.HBM) for v in (tokens, weights)])
    return packed, shares


def add_kernel(*refs):
    z = lax.axis_index("replica") // 4
    for step in range(4):
        at = lax.rem(z + step, 4)
        total = refs[0][at].astype(jnp.float32)
        for ref in refs[1:4]:
            total += ref[at].astype(jnp.float32)
        refs[4 + step][...] = total


def add_shares(shares):
    return pl.pallas_call(
        add_kernel,
        out_shape=[jax.ShapeDtypeStruct(shares[0].shape[1:], jnp.float32)] * 4,
        name="add_shares",
    )(*[pltpu.with_memory_space_constraint(v, pltpu.VMEM) for v in shares])


def place_kernel(*refs):
    z, y = lax.axis_index("replica") // 4, lax.rem(lax.axis_index("replica"), 4)
    out_ref = refs[4]
    rows = refs[0].shape[1]
    for y_step in range(4):
        for z_step in range(4):
            at = lax.rem(z + 4 - z_step, 4) * 4 + lax.rem(y + 4 - y_step, 4)
            out_ref[pl.ds(pl.multiple_of(at * rows, rows), rows), :] = refs[y_step][z_step]


def place_shares(shares):
    _, rows, out_width = shares[0].shape
    return pl.pallas_call(
        place_kernel,
        out_shape=jax.ShapeDtypeStruct((16 * rows, out_width), shares[0].dtype),
        name="place_shares",
    )(*[pltpu.with_memory_space_constraint(v, pltpu.VMEM) for v in shares])


def mask_kernel(keep_ref, mask_ref):
    mask_ref[...] = keep_ref[...].astype(mask_ref.dtype)


def mask_of(keep):
    return pl.pallas_call(
        mask_kernel,
        out_shape=jax.ShapeDtypeStruct(keep.shape, jnp.float32),
        cost_estimate=pl.CostEstimate(flops=20 * 10**9, bytes_accessed=1 << 10, transcendentals=0),
        name="mask",
    )(keep)


def project_kernel(x_ref, w0_ref, w1_ref, w2_ref, w3_ref, *out_refs):
    width = w0_ref.shape[0]
    part_width = out_refs[0].shape[2]
    for h, out_ref in enumerate(out_refs):
        total = None
        for k, w_ref in enumerate((w0_ref, w1_ref, w2_ref, w3_ref)):
            part = jnp.dot(
                x_ref[:, k * width : (k + 1) * width],
                w_ref[:, h * part_width : (h + 1) * part_width],
                preferred_element_type=jnp.float32,
            )
            total = part if total is None else total + part
        out_ref[...] = total.astype(out_ref.dtype).reshape(out_ref.shape)


def project(columns, pieces):
    shape = (PLANE, columns.shape[0] // PLANE, pieces[0].shape[1] // PARTS)
    return pl.pallas_call(
        project_kernel,
        out_shape=[jax.ShapeDtypeStruct(shape, jnp.bfloat16)] * PARTS,
        compiler_params=pltpu.CompilerParams(vmem_limit_bytes=32 << 20),
        name="project",
    )(columns, *pieces)


def gradient_kernel(slabs, columns_ref, rows_ref, *out_refs):
    width, part_width = out_refs[0].shape
    rows = rows_ref[:, :, :part_width].reshape(columns_ref.shape[0], part_width)
    for k, out_ref in zip(slabs, out_refs):
        total = lax.dot_general(
            columns_ref[:, k * width : (k + 1) * width],
            rows,
            (((0,), (0,)), ((), ())),
            preferred_element_type=jnp.float32,
        )
        out_ref[...] = total.astype(out_ref.dtype)


def gradient_of(columns, residuals, slabs, width, part_width, dtype):
    return pl.pallas_call(
        functools.partial(gradient_kernel, slabs),
        out_shape=[
            (pltpu.HBM if k == 0 else jax.ShapeDtypeStruct)((width, part_width), dtype)
            for k in slabs
        ],
        compiler_params=pltpu.CompilerParams(vmem_limit_bytes=32 << 20),
        name="gradient",
    )(columns, residuals)


def to_plane(value):
    return lax.all_to_all(value, "fsdp", 0, 0, axis_index_groups=PLANES)


def scatter_ring(blocks, beside):
    own, to_previous, to_next, far = blocks
    passing = shift_ring(far, 1)
    passing, *beside = lax.optimization_barrier((passing, *beside))
    from_next = shift_ring(to_previous.astype(jnp.bfloat16), -1)
    both = (to_next + passing.astype(jnp.float32)).astype(jnp.bfloat16)
    from_previous = shift_ring(both, 1)
    total = own + (from_previous.astype(jnp.float32) + from_next.astype(jnp.float32))
    return total, beside


def shards(weights, first_moment, second_moment, anchor, momentum, inputs, targets, keep_mask):
    initial = weights[0]
    tokens = inputs[0]
    goal_rows = targets[0]
    mask = mask_of(keep_mask)
    rows = tokens.shape[0]
    width, out_width = initial.shape
    token_count = rows * lax.axis_size("fsdp")
    workers = lax.axis_size("replica")

    packed, shares = pack(tokens, initial)
    columns = to_plane(packed).reshape(PLANE * rows, SLABS * width)
    shares[1:] = [shift_replica(shares[i], 0, i) for i in (1, 2, 3)]

    previous, following = shift_ring(initial, 1), shift_ring(initial, -1)
    previous, mask, *shares[1:2] = lax.optimization_barrier((previous, mask, *shares[1:2]))
    opposite = shift_ring(previous, 1)
    sums = add_shares(shares)
    columns, *sums = lax.optimization_barrier((columns, *sums))
    partials = list(project(columns, (initial, previous, following, opposite)))

    partials[0], *sums = lax.optimization_barrier((partials[0], *sums))
    sums[1:] = [shift_replica(sums[i], i, 0) for i in (1, 2, 3)]
    part_width = out_width // PARTS

    def residual_of(mine, h):
        goal = goal_rows[:, h * part_width : (h + 1) * part_width].astype(jnp.float32)
        projected = jnp.sum(mine.astype(jnp.float32), 0)
        residual = ((projected - goal) * mask[0][:, None] / token_count).astype(jnp.bfloat16)
        return jnp.broadcast_to(residual[None], mine.shape)

    received = to_plane(partials[0])
    out = residual_of(received, 0)
    out, *sums = lax.optimization_barrier((out, *sums))
    weight_mean = (sums[0] + sums[1] + sums[2] + sums[3]) / workers
    pseudo_grad = anchor - weight_mean
    new_momentum = NESTEROV * momentum + pseudo_grad
    new_anchor = anchor - OUTER_RATE * (pseudo_grad + NESTEROV * new_momentum)
    shared = [new_anchor] + [shift_replica(new_anchor, i, 0) for i in (1, 2, 3)]
    received = to_plane(out)
    received, *shared = lax.optimization_barrier((received, *shared))
    (far,) = gradient_of(columns, received, (3,), width, part_width, jnp.bfloat16)
    near = gradient_of(columns, received, (0, 1, 2), width, part_width, jnp.float32)
    shared = jnp.stack(shared)
    shared = [shared] + [shift_replica(shared, 0, i) for i in (1, 2, 3)]
    gradient, shared[:3] = scatter_ring((*near, far), shared[:3])
    block_anchor = place_shares(shared)

    weight_f = initial.astype(jnp.float32)
    first_new = BETA_FIRST * first_moment[0] + (1.0 - BETA_FIRST) * gradient
    second_new = BETA_SECOND * second_moment[0] + (1.0 - BETA_SECOND) * gradient * gradient
    moved = weight_f - INNER_RATE * (
        first_new / (jnp.sqrt(second_new) + EPSILON) + WEIGHT_DECAY * weight_f
    )
    inner_weight = moved.astype(jnp.bfloat16)
    mixed = ((1.0 - MIXING) * block_anchor + MIXING * inner_weight.astype(jnp.float32)).astype(
        jnp.bfloat16
    )
    return (mixed[None], first_new[None], new_anchor, new_momentum)


def solution(mesh):
    return jax.shard_map(
        shards,
        mesh=mesh,
        in_specs=(
            P("replica", "fsdp", None),
            P("replica", "fsdp", None),
            P("replica", "fsdp", None),
            P(("fsdp", "replica"), None),
            P(("fsdp", "replica"), None),
            P("replica", "fsdp", None),
            P("replica", "fsdp", None),
            P("replica", "fsdp"),
        ),
        out_specs=(
            P("replica", "fsdp", None),
            P("replica", "fsdp", None),
            P(("fsdp", "replica"), None),
            P(("fsdp", "replica"), None),
        ),
        check_vma=False,
    )
```
